32 devices in a mesh: group: 2 (over y), space: 8 (over z, x), tm: 2 (over core).
Axes of the slice: x: 2, y: 2, z: 4, core: 2. Of those that a mesh axis runs over, the one named last changes fastest.
Arguments:
- w_modes: bfloat16 [12, 1024, 768], P(('group', 'tm'), 'space'), parts along dimension 0, may hold values from -6 to 6
- v_modes: bfloat16 [12, 1024, 768], P(('group', 'tm'), 'space'), parts along dimension 0, may hold values from -6 to 6
- phase_index: int32 [1024], P('space'), may hold values from 0 to 95
- seq_offset: int32 [6], replicated, may hold values from 1 to 5
- owner_block: int32 [8], replicated, may hold values from 0 to 7, each once
Outputs:
- strips: float32 [384, 12, 768], P('space', ('group', 'tm')), parts along dimension 1
- margin: float32 [12, 768], P(('group', 'tm')), parts along dimension 0
The draws below stay inside these ranges and needn't reach their ends.
There are 2 independent parts, one for each index of `group`. The reference program is written for one: setup_inputs(seed, part) draws one part's arguments, and reference() takes and returns one part's arrays. A program takes and returns all parts, laid end to end along the dimension named above; an argument that names none is the same for every part. Nothing has to cross between parts.
Inputs may be any that keep to these rules, and one draw needn't show every extreme that they name: owner_block is a permutation of 0 to 7.
All inputs are finite; a program needn't handle non-finite values.
Results may differ from the reference program's by a relative error of at most 0.0041.
Values may be sent and summed in bfloat16 or wider, within the bound.
A program may use at most 64 MiB of HBM per device.

```python
import math
import jax
import jax.numpy as jnp
from jax import lax

NMODE = 384
MAXOFF = 5
PHASES = 96
NT = 6
SITES = 1024
OWNERS = 8
N_SPACE = 8


def touch_ends(array, own_key, least, largest):
    longest = array.shape.index(max(array.shape))
    spots = []
    for shift in (0, 1):
        where = [jax.random.randint(jax.random.fold_in(own_key, axis), (), 0, length) for axis, length in enumerate(array.shape)]
        where[longest] = (where[longest] + shift) % array.shape[longest]
        spots.append(tuple(where))
    return array.at[spots[0]].set(least).at[spots[1]].set(largest)


def shard_levels(stream_key, dims, cuts, low, high):
    gain, own = 1.0, jax.random.fold_in(stream_key, 6)
    for axis_at, parts in cuts:
        heights = jnp.exp(jax.random.uniform(jax.random.fold_in(own, axis_at), (parts,), jnp.float32, low / len(cuts), high / len(cuts)))
        gain = gain * jnp.repeat(heights, dims[axis_at] // parts).reshape([-1 if axis == axis_at else 1 for axis in range(len(dims))])
    return gain


def centred(own_key, shape, spread, reach, pieces=(), held_as=jnp.bfloat16):
    level = shard_levels(own_key, shape, pieces, -0.22, 0.18) if pieces else 1.0
    array = jax.random.normal(own_key, shape, jnp.float32) * spread * level
    return jnp.minimum(jnp.maximum(array, -reach), reach).astype(held_as)


def setup_inputs(seed: int = 0, part: int = 0) -> dict:
    key_list = jax.random.split(jax.random.key(seed), 6)
    part_splits = jax.random.split(jax.random.fold_in(key_list[5], part), 6)
    w_modes = centred(part_splits[0], (NT, SITES, 2 * NMODE), 1.0, 6.0, ((0, 2), (1, 8)))
    v_modes = centred(part_splits[1], (NT, SITES, 2 * NMODE), 1.0, 6.0, ((0, 2), (1, 8)))
    phase_index = touch_ends(jax.random.randint(key_list[2], (SITES,), 0, PHASES), jax.random.fold_in(key_list[2], 1), 0, PHASES - 1).astype(jnp.int32)
    seq_offset = touch_ends(jax.random.randint(key_list[3], (NT,), 1, MAXOFF + 1), jax.random.fold_in(key_list[3], 1), 1, MAXOFF).astype(jnp.int32)
    owner_block = jax.random.permutation(key_list[4], OWNERS).astype(jnp.int32)
    return {"w_modes": w_modes, "v_modes": v_modes, "phase_index": phase_index, "seq_offset": seq_offset, "owner_block": owner_block}


def reference(w_modes, v_modes, phase_index, seq_offset, owner_block):
    block = NMODE // N_SPACE
    scale_sites = 1.0 / math.sqrt(SITES)
    scale_modes = 1.0 / math.sqrt(2 * NMODE)
    angle = phase_index.astype(jnp.float32) * (2.0 * math.pi / PHASES)
    cosv = jnp.cos(angle)[:, None]
    sinv = jnp.sin(angle)[:, None]

    def margin_slice(pair):
        w_slice, v_slice = pair
        v_real = v_slice[:, :NMODE].astype(jnp.float32)
        v_imag = v_slice[:, NMODE:].astype(jnp.float32)
        ph_real = (cosv * v_real + sinv * v_imag).astype(jnp.bfloat16)
        ph_imag = (cosv * v_imag - sinv * v_real).astype(jnp.bfloat16)
        left = jnp.concatenate([w_slice[:, :NMODE], w_slice[:, NMODE:]], axis=0)
        right = jnp.concatenate([jnp.concatenate([ph_real, ph_imag], axis=1), jnp.concatenate([ph_imag, -ph_real], axis=1)], axis=0)
        return jnp.dot(left.T, right, preferred_element_type=jnp.float32) * scale_sites
    fields = lax.map(margin_slice, (w_modes, v_modes))
    order = (owner_block[:, None] * block + jnp.arange(block, dtype=jnp.int32)[None, :]).reshape(-1).astype(jnp.int32)
    strips = jnp.transpose(jnp.take(fields, order, axis=1), (1, 0, 2))
    rounded = fields.astype(jnp.bfloat16)
    times = jnp.arange(NT, dtype=jnp.int32)
    target = ((times + seq_offset) % NT).astype(jnp.int32)
    chosen = jnp.take(rounded, target, axis=0)

    def second_slice(triple):
        w_slice, v_slice, matrix = triple
        v_two = jnp.concatenate([jnp.concatenate([v_slice[:, :NMODE], -v_slice[:, NMODE:]], axis=1), jnp.concatenate([v_slice[:, NMODE:], v_slice[:, :NMODE]], axis=1)], axis=0)
        seq = jnp.dot(v_two, matrix.T, preferred_element_type=jnp.float32) * scale_modes
        seq_real = seq[:SITES]
        seq_imag = seq[SITES:]
        w_real = w_slice[:, :NMODE].astype(jnp.float32)
        w_imag = w_slice[:, NMODE:].astype(jnp.float32)
        over_real = lax.optimization_barrier(jnp.sum(w_real * seq_real + w_imag * seq_imag, axis=0))
        over_imag = lax.optimization_barrier(jnp.sum(w_real * seq_imag - w_imag * seq_real, axis=0))
        return jnp.concatenate([over_real, over_imag]) * scale_sites
    margin = lax.map(second_slice, (w_modes, v_modes, chosen))
    return (strips, margin)
```

```python
import functools
import math

import jax
import jax.numpy as jnp
from jax import lax
from jax.experimental import pallas as pl
from jax.experimental.pallas import tpu as pltpu
from jax.sharding import PartitionSpec as P

PHASES = 96
MESH = pl.DeviceIdType.MESH
F32 = jnp.float32
BF16 = jnp.bfloat16


def transposed_dot(left, right):
    return lax.dot_general(left, right, (((0,), (0,)), ((), ())), preferred_element_type=F32)


def kernel(
    nslices,
    w_ref, v_ref, ph_ref, seq_ref, own_ref,
    strips_ref, margin_ref,
    wx, vx, phs, phx, trig, left, right, part, tx0, tx1, rx0, rx1, fields, gfin0, gfin1, cols, tile, gathered, place, hot, chosen0, chosen1,
    xs_sem, xr_sem, zs_sem, zr_sem, ms_sem, mr_sem, ts_sem, tr_sem, as_sem, ar_sem,
):
    tdev, sdev, width = w_ref.shape
    n = width // 2
    block = strips_ref.shape[1]
    s = lax.axis_index("space")
    c = lax.axis_index("tm")
    nspace = lax.axis_size("space")
    z, x = s // 2, s % 2
    peer = 2 * z + (1 - x)
    scale_sites = 1.0 / math.sqrt(sdev * nspace)
    scale_modes = 1.0 / math.sqrt(2 * n)
    mine, other = 2 * x, 2 - 2 * x
    is_end = jnp.logical_or(z == 0, z == 3)
    is_mid = jnp.logical_not(is_end)
    low = z < 2

    barrier = pltpu.get_barrier_semaphore()
    for k in range(1, nspace):
        pl.semaphore_signal(barrier, inc=1, device_id={"space": (s + k) % nspace}, device_id_type=MESH)
    pl.semaphore_signal(barrier, inc=1, device_id={"tm": 1 - c}, device_id_type=MESH)
    phs[...] = jnp.broadcast_to(ph_ref[...].astype(F32), phs.shape)
    pl.semaphore_wait(barrier, nspace)

    def to(src, dst, ssem, rsem, **where):
        return pltpu.make_async_remote_copy(src, dst, ssem, rsem, device_id=where, device_id_type=MESH)

    swaps = [to(phs, phx, xs_sem.at[0], xr_sem.at[0], space=peer)]
    for j, t in ((0, other), (1, 1)):
        swaps.append(to(w_ref.at[t], wx.at[j], xs_sem.at[1 + 2 * j], xr_sem.at[1 + 2 * j], space=peer))
        swaps.append(to(v_ref.at[t], vx.at[j], xs_sem.at[2 + 2 * j], xr_sem.at[2 + 2 * j], space=peer))
    for swap in swaps:
        swap.start()

    def set_trig(q, row):
        angle = row * (2.0 * math.pi / PHASES)
        for k, fn in ((0, jnp.cos), (1, jnp.sin)):
            value = fn(angle)[0:1, :]
            trig[q, k] = jnp.transpose(jnp.broadcast_to(value, (sdev, sdev)))

    def build(q, w, v):
        left[:sdev] = jnp.dot(w[:, :n], hot[...], preferred_element_type=F32).astype(BF16)
        left[sdev:] = jnp.dot(w[:, n:], hot[...], preferred_element_type=F32).astype(BF16)
        for k in range(n // 128):
            lanes = slice(k * 128, (k + 1) * 128)
            vr, vi = v[:, k * 128:(k + 1) * 128], v[:, n + k * 128:n + (k + 1) * 128]
            fr, fi = vr.astype(F32), vi.astype(F32)
            cosv, sinv = trig[q, 0], trig[q, 1]
            pr = (cosv * fr + sinv * fi).astype(BF16)
            pi = (cosv * fi - sinv * fr).astype(BF16)
            for m, (re, im) in enumerate(((pr, pi), (vr, vi))):
                right[m, :sdev, lanes] = re
                right[m, :sdev, n + k * 128:n + (k + 1) * 128] = im
                right[m, sdev:, lanes] = im
                right[m, sdev:, n + k * 128:n + (k + 1) * 128] = -re

    mode = lax.broadcasted_iota(jnp.int32, (n, n), 0)
    spot = lax.broadcasted_iota(jnp.int32, (n, n), 1)
    wanted = jnp.full((n, n), -1, jnp.int32)
    for p in range(nspace):
        inside = jnp.logical_and(spot >= p * block, spot < (p + 1) * block)
        wanted = jnp.where(inside, own_ref[p] * block + spot - p * block, wanted)
    hot[...] = jnp.where(mode == wanted, 1.0, 0.0).astype(BF16)

    set_trig(0, phs[...])
    for j, t in ((0, mine), (1, 1)):
        build(0, w_ref.at[t], v_ref.at[t])
        for m in range(2):
            part[j, m] = transposed_dot(left[...], right[m]) * scale_sites

    lane = lax.broadcasted_iota(jnp.int32, (128, n), 1)
    row = lax.broadcasted_iota(jnp.int32, (128, n), 0)
    for zz in range(nspace // 2):
        first = own_ref[2 * zz] * block + row
        second = own_ref[2 * zz + 1] * block + row - block
        spot = jnp.where(row < block, first, jnp.where(row < 2 * block, second, -1))
        place[zz] = jnp.where(spot == lane, 1.0, 0.0)

    tx, rx = (tx0, tx1), (rx0, rx1)

    def rows_of(j, m, far, k):
        zd = jnp.where(low, far, 3 - far)
        at = (2 * zd + (k if j == 0 else x)) * block
        return part[j, m, pl.ds(pl.multiple_of(at, 16), block), :]

    nk = (2, 1)

    def hop(j, m, slot, dst_slot, znext):
        return to(
            tx[j].at[m, slot], rx[j].at[m, dst_slot], zs_sem.at[j, m, slot], zr_sem.at[j, m, dst_slot],
            space=2 * znext + x,
        )

    def got(j, m, slot):
        hop(j, m, 0, slot, z).wait_recv()

    inner = jnp.where(low, 1, 2)
    outer = jnp.where(low, 0, 3)

    def send(j, m, slot, dst_slot, far, znext, add):
        for k in range(nk[j]):
            value = rows_of(j, m, far, k)
            if add is not None:
                value = value + rx[j][m, add, k * block:(k + 1) * block, :].astype(F32)
            tx[j][m, slot, k * block:(k + 1) * block, :] = value.astype(BF16)
        hop(j, m, slot, dst_slot, znext).start()

    def reduce(j, m):
        @pl.when(is_end)
        def _():
            for i, far in enumerate((3, 2, 1)):
                send(j, m, i, i, far, inner, None)

        @pl.when(is_mid)
        def _():
            for i, far in enumerate((3, 2)):
                got(j, m, i)
                send(j, m, i, 3 + i, far, 3 - z, i)
            got(j, m, 3)
            send(j, m, 2, 0, 0, outer, 3)

    def finish(j, m, store):
        @pl.when(is_end)
        def _():
            got(j, m, 0)
            for k in range(nk[j]):
                store(k, rows_of(j, m, 0, k) + rx[j][m, 0, k * block:(k + 1) * block, :].astype(F32))

        @pl.when(is_mid)
        def _():
            got(j, m, 2)
            got(j, m, 4)
            for k in range(nk[j]):
                rows = slice(k * block, (k + 1) * block)
                store(k, rows_of(j, m, 1, k) + rx[j][m, 2, rows, :].astype(F32) + rx[j][m, 4, rows, :].astype(F32))

    def store_field0(k, value):
        fields[3 * c + mine, k * block:(k + 1) * block, :] = value.astype(BF16)

        @pl.when(x == k)
        def _():
            strips_ref[mine] = value

    def store_field1(k, value):
        fields[3 * c + 1, pl.ds(pl.multiple_of(x * block, 16), block), :] = value.astype(BF16)
        strips_ref[1] = value

    def store_g0(k, value):
        gfin0[k * block:(k + 1) * block, :] = value

    def store_g1(k, value):
        gfin1[...] = value

    swaps[0].wait_recv()
    set_trig(1, phx[...])
    for j in range(2):
        swaps[1 + 2 * j].wait_recv()
        swaps[2 + 2 * j].wait_recv()
        build(1, wx.at[j], vx.at[j])
        part[j, 0] += transposed_dot(left[...], right[0]) * scale_sites
        reduce(j, 0)
        part[j, 1] += transposed_dot(left[...], right[1]) * scale_sites
    for j in range(2):
        reduce(j, 1)

    half = pl.ds(pl.multiple_of(x * block, 16), block)
    half_peer = pl.ds(pl.multiple_of((1 - x) * block, 16), block)
    give0 = to(fields.at[3 * c + mine], fields.at[3 * c + mine], ms_sem.at[0], mr_sem.at[0], space=peer)
    give1 = to(fields.at[3 * c + 1, half], fields.at[3 * c + 1, half], ms_sem.at[1], mr_sem.at[1], space=peer)
    finish(0, 0, store_field0)
    give0.start()
    finish(1, 0, store_field1)
    give1.start()
    give0.wait_recv()
    give1.wait_recv()
    sibling = to(
        fields.at[pl.ds(3 * c, 3)], fields.at[pl.ds(3 * c, 3)], ts_sem.at[0], tr_sem.at[0], tm=1 - c
    )
    sibling.start()
    strips_ref[other] = fields[3 * c + other, half, :].astype(F32)
    sibling.wait_recv()

    def weight(t, k):
        at = 3 * c + t
        there = at + seq_ref[at]
        return jnp.where(jnp.logical_or(there == k, there == k + nslices), 1.0, 0.0)

    chosen0[...] = sum(weight(mine, k) * fields[k].astype(F32) for k in range(nslices))
    chosen1[...] = sum(weight(1, k) * fields[k, half, :].astype(F32) for k in range(nslices))
    finish(0, 1, store_g0)
    finish(1, 1, store_g1)

    def margins(g, field):
        gr, gi = g[:, :n], g[:, n:]
        mr, mi = field[:, :n], field[:, n:]
        re = jnp.sum(mr * gr - mi * gi, axis=1, keepdims=True) * scale_modes
        im = jnp.sum(mr * gi + mi * gr, axis=1, keepdims=True) * scale_modes
        return re, im

    cols[...] = jnp.zeros_like(cols)
    at = lax.broadcasted_iota(jnp.int32, (2 * block, 128), 1)
    re, im = margins(gfin0[...], chosen0[...])
    cols[:2 * block] = jnp.where(at == 0, re, 0.0) + jnp.where(at == 1, im, 0.0)
    re, im = margins(gfin1[...], chosen1[...])
    at = lax.broadcasted_iota(jnp.int32, (block, 128), 1)
    cols[half] += jnp.where(at == 2, re, 0.0) + jnp.where(at == 3, im, 0.0)
    tile[...] = jnp.transpose(cols[...])[:8]

    shares = []
    for k in range(1, nspace):
        share = to(tile, gathered.at[s], as_sem.at[k], ar_sem.at[s], space=(s + k) % nspace)
        share.start()
        shares.append(share)
    gathered[s] = tile[...]
    for k in range(1, nspace):
        origin = (s + k) % nspace
        to(tile, gathered.at[origin], as_sem.at[k], ar_sem.at[origin], space=origin).wait_recv()
    total = jnp.zeros((16, n), F32)
    for zz in range(nspace // 2):
        both = jnp.concatenate([gathered[2 * zz], gathered[2 * zz + 1]], axis=0)
        total += jnp.dot(both, place[zz], precision=lax.Precision.HIGHEST, preferred_element_type=F32)
    margin_ref[0:1, :n] = total[0:1]
    margin_ref[0:1, n:] = total[1:2]
    margin_ref[1:2, :n] = total[2:3] + total[10:11]
    margin_ref[1:2, n:] = total[3:4] + total[11:12]
    margin_ref[2:3, :n] = total[8:9]
    margin_ref[2:3, n:] = total[9:10]

    for swap in swaps:
        swap.wait_send()
    for j in range(2):
        for m in range(2):
            for slot in range(3):
                hop(j, m, slot, 0, z).wait_send()
    give0.wait_send()
    give1.wait_send()
    sibling.wait_send()
    for share in shares:
        share.wait_send()


def fused(w_modes, v_modes, phase_index, seq_offset, owner_block):
    tdev, sdev, width = w_modes.shape
    n = width // 2
    nspace = lax.axis_size("space")
    ntm = lax.axis_size("tm")
    block = n // nspace
    vmem = pl.BlockSpec(memory_space=pltpu.VMEM)
    smem = pl.BlockSpec(memory_space=pltpu.SMEM)
    dma = pltpu.SemaphoreType.DMA
    strips, margin = pl.pallas_call(
        functools.partial(kernel, tdev * ntm),
        out_shape=(
            jax.ShapeDtypeStruct((tdev, block, width), F32),
            jax.ShapeDtypeStruct((tdev, width), F32),
        ),
        in_specs=[vmem, vmem, vmem, smem, smem],
        out_specs=(vmem, vmem),
        scratch_shapes=[
            pltpu.VMEM((2, sdev, width), BF16),
            pltpu.VMEM((2, sdev, width), BF16),
            pltpu.VMEM((8, sdev), F32),
            pltpu.VMEM((8, sdev), F32),
            pltpu.VMEM((2, 2, sdev, sdev), F32),
            pltpu.VMEM((2 * sdev, n), BF16),
            pltpu.VMEM((2, 2 * sdev, width), BF16),
            pltpu.VMEM((2, 2, n, width), F32),
            pltpu.VMEM((2, 3, 2 * block, width), BF16),
            pltpu.VMEM((2, 3, block, width), BF16),
            pltpu.VMEM((2, 5, 2 * block, width), BF16),
            pltpu.VMEM((2, 5, block, width), BF16),
            pltpu.VMEM((tdev * ntm, 2 * block, width), BF16),
            pltpu.VMEM((2 * block, width), F32),
            pltpu.VMEM((block, width), F32),
            pltpu.VMEM((128, 128), F32),
            pltpu.VMEM((8, 128), F32),
            pltpu.VMEM((nspace, 8, 128), F32),
            pltpu.VMEM((nspace // 2, 128, n), F32),
            pltpu.VMEM((n, n), BF16),
            pltpu.VMEM((2 * block, width), F32),
            pltpu.VMEM((block, width), F32),
            dma((5,)),
            dma((5,)),
            dma((2, 2, 3)),
            dma((2, 2, 5)),
            dma((2,)),
            dma((2,)),
            dma((1,)),
            dma((1,)),
            dma((nspace,)),
            dma((nspace,)),
        ],
        compiler_params=pltpu.CompilerParams(
            collective_id=0, has_side_effects=True, vmem_limit_bytes=48 * 1024 * 1024
        ),
        cost_estimate=pl.CostEstimate(
            flops=16 * tdev * sdev * n * n, bytes_accessed=4 * tdev * sdev * width, transcendentals=0
        ),
    )(w_modes, v_modes, phase_index.reshape(1, sdev), seq_offset, owner_block)
    return jnp.transpose(strips, (1, 0, 2)), margin


def plain(w_modes, v_modes, phase_index, seq_offset, owner_block):
    tdev, sdev, width = w_modes.shape
    nmode = width // 2
    nspace = lax.axis_size("space")
    ntm = lax.axis_size("tm")
    block = nmode // nspace
    total_slices = tdev * ntm
    scale_sites = 1.0 / math.sqrt(sdev * nspace)
    scale_modes = 1.0 / math.sqrt(2 * nmode)
    order = (owner_block[:, None] * block + jnp.arange(block, dtype=jnp.int32)[None, :]).reshape(-1)
    spots = order[:, None] == jnp.arange(nmode, dtype=jnp.int32)[None, :]
    hot = spots.astype(BF16)
    exact = spots.astype(F32)
    w_real = jnp.einsum("tsm,km->tsk", w_modes[:, :, :nmode], hot)
    w_imag = jnp.einsum("tsm,km->tsk", w_modes[:, :, nmode:], hot)
    v_real, v_imag = v_modes[:, :, :nmode], v_modes[:, :, nmode:]
    left = jnp.concatenate([w_real, w_imag], axis=1)
    angle = phase_index.astype(F32) * (2.0 * math.pi / PHASES)
    cosv = jnp.cos(angle)[None, :, None]
    sinv = jnp.sin(angle)[None, :, None]
    fr, fi = v_real.astype(F32), v_imag.astype(F32)
    ph_real = (cosv * fr + sinv * fi).astype(BF16)
    ph_imag = (cosv * fi - sinv * fr).astype(BF16)

    def field(real, imag):
        right = jnp.concatenate(
            [jnp.concatenate([real, imag], axis=2), jnp.concatenate([imag, -real], axis=2)], axis=1
        )
        sums = jnp.einsum("tsi,tsj->itj", left, right, preferred_element_type=F32) * scale_sites
        return lax.psum_scatter(sums, "space", scatter_dimension=0, tiled=True)

    strips = field(ph_real, ph_imag)
    g = field(v_real, v_imag)
    rounded = strips.astype(BF16)
    both = lax.all_gather(rounded, "tm", axis=1, tiled=True)
    mine = lax.axis_index("tm") * tdev + jnp.arange(tdev, dtype=jnp.int32)
    every = jnp.arange(total_slices, dtype=jnp.int32)
    offset = jnp.sum(jnp.where(mine[:, None] == every[None, :], seq_offset[None, :], 0), axis=1)
    target = (mine + offset) % total_slices
    pick = (target[:, None] == every[None, :]).astype(BF16)
    chosen = jnp.einsum("iaj,ta->itj", both, pick, preferred_element_type=F32)
    cr, ci = chosen[:, :, :nmode], chosen[:, :, nmode:]
    gr, gi = g[:, :, :nmode], g[:, :, nmode:]
    over = jnp.concatenate(
        [jnp.sum(cr * gr - ci * gi, axis=2), jnp.sum(cr * gi + ci * gr, axis=2)], axis=1
    ) * scale_modes
    rows = lax.all_gather(over, "space", axis=0, tiled=True)
    margin = jnp.einsum("kt,km->tm", rows, exact, precision=lax.Precision.HIGHEST)
    return strips, jnp.concatenate([margin[:tdev], margin[tdev:]], axis=1)


def shards(w_modes, v_modes, phase_index, seq_offset, owner_block):
    tdev, sdev, width = w_modes.shape
    nmode = width // 2
    nspace = lax.axis_size("space")
    fits = (
        tdev == 3 and lax.axis_size("tm") == 2 and nspace == 8 and sdev == 128
        and nmode % 128 == 0 and (nmode // nspace) % 16 == 0 and 2 * (nmode // nspace) <= 128
    )
    return (fused if fits else plain)(w_modes, v_modes, phase_index, seq_offset, owner_block)


def solution(mesh):
    in_specs = (
        P(("group", "tm"), "space", None),
        P(("group", "tm"), "space", None),
        P("space"),
        P(),
        P(),
    )
    out_specs = (P("space", ("group", "tm"), None), P(("group", "tm"), None))
    return jax.shard_map(shards, mesh=mesh, in_specs=in_specs, out_specs=out_specs, check_vma=False)
```

```python
import functools
import math

import jax
import jax.numpy as jnp
from jax import lax
from jax.experimental import pallas as pl
from jax.experimental.pallas import tpu as pltpu
from jax.sharding import PartitionSpec as P

PHASES = 96
MESH = pl.DeviceIdType.MESH
F32 = jnp.float32
BF16 = jnp.bfloat16


def transposed_dot(left, right):
    return lax.dot_general(left, right, (((0,), (0,)), ((), ())), preferred_element_type=F32)


def kernel(
    nslices,
    w_ref, v_ref, ph_ref, seq_ref, own_ref,
    strips_ref, margin_ref,
    wx, vx, phs, phx, trig, left, right, part, tx0, tx1, rx0, rx1, fields, gfin0, gfin1, cols, tile, gathered, place, hot, chosen0, chosen1, wo, vo, lo_sem,
    xs_sem, xr_sem, zs_sem, zr_sem, ms_sem, mr_sem, ts_sem, tr_sem, as_sem, ar_sem,
):
    tdev, sdev, width = w_ref.shape
    n = width // 2
    block = strips_ref.shape[1]
    s = lax.axis_index("space")
    c = lax.axis_index("tm")
    nspace = lax.axis_size("space")
    z, x = s // 2, s % 2
    peer = 2 * z + (1 - x)
    scale_sites = 1.0 / math.sqrt(sdev * nspace)
    scale_modes = 1.0 / math.sqrt(2 * n)
    mine, other = 2 * x, 2 - 2 * x
    is_end = jnp.logical_or(z == 0, z == 3)
    is_mid = jnp.logical_not(is_end)
    low = z < 2

    loads = []
    for j, t in ((0, mine), (1, 1)):
        loads.append(pltpu.make_async_copy(w_ref.at[t], wo.at[j], lo_sem.at[2 * j]))
        loads.append(pltpu.make_async_copy(v_ref.at[t], vo.at[j], lo_sem.at[2 * j + 1]))
    for load in loads:
        load.start()

    barrier = pltpu.get_barrier_semaphore()
    for k in range(1, nspace):
        pl.semaphore_signal(barrier, inc=1, device_id={"space": (s + k) % nspace}, device_id_type=MESH)
    pl.semaphore_signal(barrier, inc=1, device_id={"tm": 1 - c}, device_id_type=MESH)
    phs[...] = jnp.broadcast_to(ph_ref[...].astype(F32), phs.shape)
    pl.semaphore_wait(barrier, nspace)

    def to(src, dst, ssem, rsem, **where):
        return pltpu.make_async_remote_copy(src, dst, ssem, rsem, device_id=where, device_id_type=MESH)

    swaps = [to(phs, phx, xs_sem.at[0], xr_sem.at[0], space=peer)]
    for j, t in ((0, other), (1, 1)):
        swaps.append(to(w_ref.at[t], wx.at[j], xs_sem.at[1 + 2 * j], xr_sem.at[1 + 2 * j], space=peer))
        swaps.append(to(v_ref.at[t], vx.at[j], xs_sem.at[2 + 2 * j], xr_sem.at[2 + 2 * j], space=peer))
    for swap in swaps[:3]:
        swap.start()

    def set_trig(q, row):
        angle = row * (2.0 * math.pi / PHASES)
        for k, fn in ((0, jnp.cos), (1, jnp.sin)):
            value = fn(angle)[0:1, :]
            trig[q, k] = jnp.transpose(jnp.broadcast_to(value, (sdev, sdev)))

    def build(q, w, v):
        left[:sdev] = jnp.dot(w[:, :n], hot[...], preferred_element_type=F32).astype(BF16)
        left[sdev:] = jnp.dot(w[:, n:], hot[...], preferred_element_type=F32).astype(BF16)
        for k in range(n // 128):
            lanes = slice(k * 128, (k + 1) * 128)
            vr, vi = v[:, k * 128:(k + 1) * 128], v[:, n + k * 128:n + (k + 1) * 128]
            fr, fi = vr.astype(F32), vi.astype(F32)
            cosv, sinv = trig[q, 0], trig[q, 1]
            pr = (cosv * fr + sinv * fi).astype(BF16)
            pi = (cosv * fi - sinv * fr).astype(BF16)
            for m, (re, im) in enumerate(((pr, pi), (vr, vi))):
                right[m, :sdev, lanes] = re
                right[m, :sdev, n + k * 128:n + (k + 1) * 128] = im
                right[m, sdev:, lanes] = im
                right[m, sdev:, n + k * 128:n + (k + 1) * 128] = -re

    mode = lax.broadcasted_iota(jnp.int32, (n, n), 0)
    spot = lax.broadcasted_iota(jnp.int32, (n, n), 1)
    wanted = jnp.full((n, n), -1, jnp.int32)
    for p in range(nspace):
        inside = jnp.logical_and(spot >= p * block, spot < (p + 1) * block)
        wanted = jnp.where(inside, own_ref[p] * block + spot - p * block, wanted)
    hot[...] = jnp.where(mode == wanted, 1.0, 0.0).astype(BF16)

    set_trig(0, phs[...])
    for j in range(2):
        loads[2 * j].wait()
        loads[2 * j + 1].wait()
        build(0, wo.at[j], vo.at[j])
        for m in range(2):
            part[j, m] = transposed_dot(left[...], right[m]) * scale_sites

    lane = lax.broadcasted_iota(jnp.int32, (128, n), 1)
    row = lax.broadcasted_iota(jnp.int32, (128, n), 0)
    for zz in range(nspace // 2):
        first = own_ref[2 * zz] * block + row
        second = own_ref[2 * zz + 1] * block + row - block
        spot = jnp.where(row < block, first, jnp.where(row < 2 * block, second, -1))
        place[zz] = jnp.where(spot == lane, 1.0, 0.0)

    tx, rx = (tx0, tx1), (rx0, rx1)

    def rows_of(j, m, far, k):
        zd = jnp.where(low, far, 3 - far)
        at = (2 * zd + (k if j == 0 else x)) * block
        return part[j, m, pl.ds(pl.multiple_of(at, 16), block), :]

    nk = (2, 1)

    def hop(j, m, slot, dst_slot, znext):
        return to(
            tx[j].at[m, slot], rx[j].at[m, dst_slot], zs_sem.at[j, m, slot], zr_sem.at[j, m, dst_slot],
            space=2 * znext + x,
        )

    def got(j, m, slot):
        hop(j, m, 0, slot, z).wait_recv()

    inner = jnp.where(low, 1, 2)
    outer = jnp.where(low, 0, 3)

    def send(j, m, slot, dst_slot, far, znext, add):
        for k in range(nk[j]):
            value = rows_of(j, m, far, k)
            if add is not None:
                value = value + rx[j][m, add, k * block:(k + 1) * block, :].astype(F32)
            tx[j][m, slot, k * block:(k + 1) * block, :] = value.astype(BF16)
        hop(j, m, slot, dst_slot, znext).start()

    def reduce(j, m):
        @pl.when(is_end)
        def _():
            for i, far in enumerate((3, 2, 1)):
                send(j, m, i, i, far, inner, None)

        @pl.when(is_mid)
        def _():
            for i, far in enumerate((3, 2)):
                got(j, m, i)
                send(j, m, i, 3 + i, far, 3 - z, i)
            got(j, m, 3)
            send(j, m, 2, 0, 0, outer, 3)

    def finish(j, m, store):
        @pl.when(is_end)
        def _():
            got(j, m, 0)
            for k in range(nk[j]):
                store(k, rows_of(j, m, 0, k) + rx[j][m, 0, k * block:(k + 1) * block, :].astype(F32))

        @pl.when(is_mid)
        def _():
            got(j, m, 2)
            got(j, m, 4)
            for k in range(nk[j]):
                rows = slice(k * block, (k + 1) * block)
                store(k, rows_of(j, m, 1, k) + rx[j][m, 2, rows, :].astype(F32) + rx[j][m, 4, rows, :].astype(F32))

    def store_field0(k, value):
        fields[3 * c + mine, k * block:(k + 1) * block, :] = value.astype(BF16)

        @pl.when(x == k)
        def _():
            strips_ref[mine] = value

    def store_field1(k, value):
        fields[3 * c + 1, pl.ds(pl.multiple_of(x * block, 16), block), :] = value.astype(BF16)
        strips_ref[1] = value

    def store_g0(k, value):
        gfin0[k * block:(k + 1) * block, :] = value

    def store_g1(k, value):
        gfin1[...] = value

    for swap in swaps[:3]:
        swap.wait_send()
    for swap in swaps[3:]:
        swap.start()
    swaps[0].wait_recv()
    set_trig(1, phx[...])
    for j in range(2):
        swaps[1 + 2 * j].wait_recv()
        swaps[2 + 2 * j].wait_recv()
        build(1, wx.at[j], vx.at[j])
        part[j, 0] += transposed_dot(left[...], right[0]) * scale_sites
        reduce(j, 0)
        part[j, 1] += transposed_dot(left[...], right[1]) * scale_sites
    for j in range(2):
        reduce(j, 1)

    half = pl.ds(pl.multiple_of(x * block, 16), block)
    half_peer = pl.ds(pl.multiple_of((1 - x) * block, 16), block)
    give0 = to(fields.at[3 * c + mine], fields.at[3 * c + mine], ms_sem.at[0], mr_sem.at[0], space=peer)
    give1 = to(fields.at[3 * c + 1, half], fields.at[3 * c + 1, half], ms_sem.at[1], mr_sem.at[1], space=peer)
    finish(0, 0, store_field0)
    give0.start()
    finish(1, 0, store_field1)
    give1.start()
    give0.wait_recv()
    give1.wait_recv()
    sibling = to(
        fields.at[pl.ds(3 * c, 3)], fields.at[pl.ds(3 * c, 3)], ts_sem.at[0], tr_sem.at[0], tm=1 - c
    )
    sibling.start()
    strips_ref[other] = fields[3 * c + other, half, :].astype(F32)
    sibling.wait_recv()

    def weight(t, k):
        at = 3 * c + t
        there = at + seq_ref[at]
        return jnp.where(jnp.logical_or(there == k, there == k + nslices), 1.0, 0.0)

    chosen0[...] = sum(weight(mine, k) * fields[k].astype(F32) for k in range(nslices))
    chosen1[...] = sum(weight(1, k) * fields[k, half, :].astype(F32) for k in range(nslices))
    finish(0, 1, store_g0)
    finish(1, 1, store_g1)

    def margins(g, field):
        gr, gi = g[:, :n], g[:, n:]
        mr, mi = field[:, :n], field[:, n:]
        re = jnp.sum(mr * gr - mi * gi, axis=1, keepdims=True) * scale_modes
        im = jnp.sum(mr * gi + mi * gr, axis=1, keepdims=True) * scale_modes
        return re, im

    cols[...] = jnp.zeros_like(cols)
    at = lax.broadcasted_iota(jnp.int32, (2 * block, 128), 1)
    re, im = margins(gfin0[...], chosen0[...])
    cols[:2 * block] = jnp.where(at == 0, re, 0.0) + jnp.where(at == 1, im, 0.0)
    re, im = margins(gfin1[...], chosen1[...])
    at = lax.broadcasted_iota(jnp.int32, (block, 128), 1)
    cols[half] += jnp.where(at == 2, re, 0.0) + jnp.where(at == 3, im, 0.0)
    tile[...] = jnp.transpose(cols[...])[:8]

    shares = []
    for k in range(1, nspace):
        share = to(tile, gathered.at[s], as_sem.at[k], ar_sem.at[s], space=(s + k) % nspace)
        share.start()
        shares.append(share)
    gathered[s] = tile[...]
    for k in range(1, nspace):
        origin = (s + k) % nspace
        to(tile, gathered.at[origin], as_sem.at[k], ar_sem.at[origin], space=origin).wait_recv()
    total = jnp.zeros((16, n), F32)
    for zz in range(nspace // 2):
        both = jnp.concatenate([gathered[2 * zz], gathered[2 * zz + 1]], axis=0)
        total += jnp.dot(both, place[zz], precision=lax.Precision.HIGHEST, preferred_element_type=F32)
    margin_ref[0:1, :n] = total[0:1]
    margin_ref[0:1, n:] = total[1:2]
    margin_ref[1:2, :n] = total[2:3] + total[10:11]
    margin_ref[1:2, n:] = total[3:4] + total[11:12]
    margin_ref[2:3, :n] = total[8:9]
    margin_ref[2:3, n:] = total[9:10]

    for swap in swaps[3:]:
        swap.wait_send()
    for j in range(2):
        for m in range(2):
            for slot in range(3):
                hop(j, m, slot, 0, z).wait_send()
    give0.wait_send()
    give1.wait_send()
    sibling.wait_send()
    for share in shares:
        share.wait_send()


def fused(w_modes, v_modes, phase_index, seq_offset, owner_block):
    tdev, sdev, width = w_modes.shape
    n = width // 2
    nspace = lax.axis_size("space")
    ntm = lax.axis_size("tm")
    block = n // nspace
    vmem = pl.BlockSpec(memory_space=pltpu.VMEM)
    hbm = pl.BlockSpec(memory_space=pltpu.HBM)
    smem = pl.BlockSpec(memory_space=pltpu.SMEM)
    dma = pltpu.SemaphoreType.DMA
    strips, margin = pl.pallas_call(
        functools.partial(kernel, tdev * ntm),
        out_shape=(
            jax.ShapeDtypeStruct((tdev, block, width), F32),
            jax.ShapeDtypeStruct((tdev, width), F32),
        ),
        in_specs=[hbm, hbm, vmem, smem, smem],
        out_specs=(vmem, vmem),
        scratch_shapes=[
            pltpu.VMEM((2, sdev, width), BF16),
            pltpu.VMEM((2, sdev, width), BF16),
            pltpu.VMEM((8, sdev), F32),
            pltpu.VMEM((8, sdev), F32),
            pltpu.VMEM((2, 2, sdev, sdev), F32),
            pltpu.VMEM((2 * sdev, n), BF16),
            pltpu.VMEM((2, 2 * sdev, width), BF16),
            pltpu.VMEM((2, 2, n, width), F32),
            pltpu.VMEM((2, 3, 2 * block, width), BF16),
            pltpu.VMEM((2, 3, block, width), BF16),
            pltpu.VMEM((2, 5, 2 * block, width), BF16),
            pltpu.VMEM((2, 5, block, width), BF16),
            pltpu.VMEM((tdev * ntm, 2 * block, width), BF16),
            pltpu.VMEM((2 * block, width), F32),
            pltpu.VMEM((block, width), F32),
            pltpu.VMEM((128, 128), F32),
            pltpu.VMEM((8, 128), F32),
            pltpu.VMEM((nspace, 8, 128), F32),
            pltpu.VMEM((nspace // 2, 128, n), F32),
            pltpu.VMEM((n, n), BF16),
            pltpu.VMEM((2 * block, width), F32),
            pltpu.VMEM((block, width), F32),
            pltpu.VMEM((2, sdev, width), BF16),
            pltpu.VMEM((2, sdev, width), BF16),
            dma((4,)),
            dma((5,)),
            dma((5,)),
            dma((2, 2, 3)),
            dma((2, 2, 5)),
            dma((2,)),
            dma((2,)),
            dma((1,)),
            dma((1,)),
            dma((nspace,)),
            dma((nspace,)),
        ],
        compiler_params=pltpu.CompilerParams(
            collective_id=0, has_side_effects=True, vmem_limit_bytes=48 * 1024 * 1024
        ),
        cost_estimate=pl.CostEstimate(
            flops=16 * tdev * sdev * n * n, bytes_accessed=4 * tdev * sdev * width, transcendentals=0
        ),
    )(w_modes, v_modes, phase_index.reshape(1, sdev), seq_offset, owner_block)
    return jnp.transpose(strips, (1, 0, 2)), margin


def plain(w_modes, v_modes, phase_index, seq_offset, owner_block):
    tdev, sdev, width = w_modes.shape
    nmode = width // 2
    nspace = lax.axis_size("space")
    ntm = lax.axis_size("tm")
    block = nmode // nspace
    total_slices = tdev * ntm
    scale_sites = 1.0 / math.sqrt(sdev * nspace)
    scale_modes = 1.0 / math.sqrt(2 * nmode)
    order = (owner_block[:, None] * block + jnp.arange(block, dtype=jnp.int32)[None, :]).reshape(-1)
    spots = order[:, None] == jnp.arange(nmode, dtype=jnp.int32)[None, :]
    hot = spots.astype(BF16)
    exact = spots.astype(F32)
    w_real = jnp.einsum("tsm,km->tsk", w_modes[:, :, :nmode], hot)
    w_imag = jnp.einsum("tsm,km->tsk", w_modes[:, :, nmode:], hot)
    v_real, v_imag = v_modes[:, :, :nmode], v_modes[:, :, nmode:]
    left = jnp.concatenate([w_real, w_imag], axis=1)
    angle = phase_index.astype(F32) * (2.0 * math.pi / PHASES)
    cosv = jnp.cos(angle)[None, :, None]
    sinv = jnp.sin(angle)[None, :, None]
    fr, fi = v_real.astype(F32), v_imag.astype(F32)
    ph_real = (cosv * fr + sinv * fi).astype(BF16)
    ph_imag = (cosv * fi - sinv * fr).astype(BF16)

    def field(real, imag):
        right = jnp.concatenate(
            [jnp.concatenate([real, imag], axis=2), jnp.concatenate([imag, -real], axis=2)], axis=1
        )
        sums = jnp.einsum("tsi,tsj->itj", left, right, preferred_element_type=F32) * scale_sites
        return lax.psum_scatter(sums, "space", scatter_dimension=0, tiled=True)

    strips = field(ph_real, ph_imag)
    g = field(v_real, v_imag)
    rounded = strips.astype(BF16)
    both = lax.all_gather(rounded, "tm", axis=1, tiled=True)
    mine = lax.axis_index("tm") * tdev + jnp.arange(tdev, dtype=jnp.int32)
    every = jnp.arange(total_slices, dtype=jnp.int32)
    offset = jnp.sum(jnp.where(mine[:, None] == every[None, :], seq_offset[None, :], 0), axis=1)
    target = (mine + offset) % total_slices
    pick = (target[:, None] == every[None, :]).astype(BF16)
    chosen = jnp.einsum("iaj,ta->itj", both, pick, preferred_element_type=F32)
    cr, ci = chosen[:, :, :nmode], chosen[:, :, nmode:]
    gr, gi = g[:, :, :nmode], g[:, :, nmode:]
    over = jnp.concatenate(
        [jnp.sum(cr * gr - ci * gi, axis=2), jnp.sum(cr * gi + ci * gr, axis=2)], axis=1
    ) * scale_modes
    rows = lax.all_gather(over, "space", axis=0, tiled=True)
    margin = jnp.einsum("kt,km->tm", rows, exact, precision=lax.Precision.HIGHEST)
    return strips, jnp.concatenate([margin[:tdev], margin[tdev:]], axis=1)


def shards(w_modes, v_modes, phase_index, seq_offset, owner_block):
    tdev, sdev, width = w_modes.shape
    nmode = width // 2
    nspace = lax.axis_size("space")
    fits = (
        tdev == 3 and lax.axis_size("tm") == 2 and nspace == 8 and sdev == 128
        and nmode % 128 == 0 and (nmode // nspace) % 16 == 0 and 2 * (nmode // nspace) <= 128
    )
    return (fused if fits else plain)(w_modes, v_modes, phase_index, seq_offset, owner_block)


def solution(mesh):
    in_specs = (
        P(("group", "tm"), "space", None),
        P(("group", "tm"), "space", None),
        P("space"),
        P(),
        P(),
    )
    out_specs = (P("space", ("group", "tm"), None), P(("group", "tm"), None))
    return jax.shard_map(shards, mesh=mesh, in_specs=in_specs, out_specs=out_specs, check_vma=False)
```

```python
import functools
import math

import jax
import jax.numpy as jnp
from jax import lax
from jax.experimental import pallas as pl
from jax.experimental.pallas import tpu as pltpu
from jax.sharding import PartitionSpec as P

PHASES = 96
MESH = pl.DeviceIdType.MESH
F32 = jnp.float32
BF16 = jnp.bfloat16


def transposed_dot(left, right):
    return lax.dot_general(left, right, (((0,), (0,)), ((), ())), preferred_element_type=F32)


def kernel(
    nslices,
    w_ref, v_ref, ph_ref, seq_ref, own_ref,
    strips_ref, margin_ref,
    wx, vx, phs, phx, trig, left, right, part, tx0, tx1, rx0, rx1, fields, gfin0, gfin1, cols, tile, gathered, place, hot, chosen0, chosen1, wo, vo, lo_sem,
    xs_sem, xr_sem, zs_sem, zr_sem, ms_sem, mr_sem, ts_sem, tr_sem, as_sem, ar_sem,
):
    tdev, sdev, width = w_ref.shape
    n = width // 2
    block = strips_ref.shape[1]
    s = lax.axis_index("space")
    c = lax.axis_index("tm")
    nspace = lax.axis_size("space")
    z, x = s // 2, s % 2
    peer = 2 * z + (1 - x)
    scale_sites = 1.0 / math.sqrt(sdev * nspace)
    scale_modes = 1.0 / math.sqrt(2 * n)
    mine, other = 2 * x, 2 - 2 * x
    is_end = jnp.logical_or(z == 0, z == 3)
    is_mid = jnp.logical_not(is_end)
    low = z < 2

    loads = []
    for j, t in ((0, mine), (1, 1)):
        loads.append(pltpu.make_async_copy(w_ref.at[t], wo.at[j], lo_sem.at[2 * j]))
        loads.append(pltpu.make_async_copy(v_ref.at[t], vo.at[j], lo_sem.at[2 * j + 1]))
    for load in loads:
        load.start()

    barrier = pltpu.get_barrier_semaphore()
    for k in range(1, nspace):
        pl.semaphore_signal(barrier, inc=1, device_id={"space": (s + k) % nspace}, device_id_type=MESH)
    pl.semaphore_signal(barrier, inc=1, device_id={"tm": 1 - c}, device_id_type=MESH)
    phs[...] = jnp.broadcast_to(ph_ref[...].astype(F32), phs.shape)
    pl.semaphore_wait(barrier, nspace)

    def to(src, dst, ssem, rsem, **where):
        return pltpu.make_async_remote_copy(src, dst, ssem, rsem, device_id=where, device_id_type=MESH)

    swaps = [to(phs, phx, xs_sem.at[0], xr_sem.at[0], space=peer)]
    for j, t in ((0, other), (1, 1)):
        swaps.append(to(w_ref.at[t], wx.at[j], xs_sem.at[1 + 2 * j], xr_sem.at[1 + 2 * j], space=peer))
        swaps.append(to(v_ref.at[t], vx.at[j], xs_sem.at[2 + 2 * j], xr_sem.at[2 + 2 * j], space=peer))
    for swap in swaps:
        swap.start()

    def set_trig(q, row):
        angle = row * (2.0 * math.pi / PHASES)
        for k, fn in ((0, jnp.cos), (1, jnp.sin)):
            value = fn(angle)[0:1, :]
            trig[q, k] = jnp.transpose(jnp.broadcast_to(value, (sdev, sdev)))

    def build(q, w, v):
        left[:sdev] = jnp.dot(w[:, :n], hot[...], preferred_element_type=F32).astype(BF16)
        left[sdev:] = jnp.dot(w[:, n:], hot[...], preferred_element_type=F32).astype(BF16)
        for k in range(n // 128):
            lanes = slice(k * 128, (k + 1) * 128)
            vr, vi = v[:, k * 128:(k + 1) * 128], v[:, n + k * 128:n + (k + 1) * 128]
            fr, fi = vr.astype(F32), vi.astype(F32)
            cosv, sinv = trig[q, 0], trig[q, 1]
            pr = (cosv * fr + sinv * fi).astype(BF16)
            pi = (cosv * fi - sinv * fr).astype(BF16)
            for m, (re, im) in enumerate(((pr, pi), (vr, vi))):
                right[m, :sdev, lanes] = re
                right[m, :sdev, n + k * 128:n + (k + 1) * 128] = im
                right[m, sdev:, lanes] = im
                right[m, sdev:, n + k * 128:n + (k + 1) * 128] = -re

    mode = lax.broadcasted_iota(jnp.int32, (n, n), 0)
    spot = lax.broadcasted_iota(jnp.int32, (n, n), 1)
    wanted = jnp.full((n, n), -1, jnp.int32)
    for p in range(nspace):
        inside = jnp.logical_and(spot >= p * block, spot < (p + 1) * block)
        wanted = jnp.where(inside, own_ref[p] * block + spot - p * block, wanted)
    hot[...] = jnp.where(mode == wanted, 1.0, 0.0).astype(BF16)

    set_trig(0, phs[...])
    for j in range(2):
        loads[2 * j].wait()
        loads[2 * j + 1].wait()
        build(0, wo.at[j], vo.at[j])
        for m in range(2):
            part[j, m] = transposed_dot(left[...], right[m]) * scale_sites

    lane = lax.broadcasted_iota(jnp.int32, (128, n), 1)
    row = lax.broadcasted_iota(jnp.int32, (128, n), 0)
    for zz in range(nspace // 2):
        first = own_ref[2 * zz] * block + row
        second = own_ref[2 * zz + 1] * block + row - block
        spot = jnp.where(row < block, first, jnp.where(row < 2 * block, second, -1))
        place[zz] = jnp.where(spot == lane, 1.0, 0.0)

    tx, rx = (tx0, tx1), (rx0, rx1)

    def rows_of(j, m, far, k):
        zd = jnp.where(low, far, 3 - far)
        at = (2 * zd + (k if j == 0 else x)) * block
        return part[j, m, pl.ds(pl.multiple_of(at, 16), block), :]

    nk = (2, 1)

    def hop(j, m, slot, dst_slot, znext):
        return to(
            tx[j].at[m, slot], rx[j].at[m, dst_slot], zs_sem.at[j, m, slot], zr_sem.at[j, m, dst_slot],
            space=2 * znext + x,
        )

    def got(j, m, slot):
        hop(j, m, 0, slot, z).wait_recv()

    inner = jnp.where(low, 1, 2)
    outer = jnp.where(low, 0, 3)

    def send(j, m, slot, dst_slot, far, znext, add):
        for k in range(nk[j]):
            value = rows_of(j, m, far, k)
            if add is not None:
                value = value + rx[j][m, add, k * block:(k + 1) * block, :].astype(F32)
            tx[j][m, slot, k * block:(k + 1) * block, :] = value.astype(BF16)
        hop(j, m, slot, dst_slot, znext).start()

    def reduce_end(j, m):
        @pl.when(is_end)
        def _():
            for i, far in enumerate((3, 2, 1)):
                send(j, m, i, i, far, inner, None)

    def reduce_mid(j, m):
        @pl.when(is_mid)
        def _():
            for i, far in enumerate((3, 2)):
                got(j, m, i)
                send(j, m, i, 3 + i, far, 3 - z, i)
            got(j, m, 3)
            send(j, m, 2, 0, 0, outer, 3)

    def finish(j, m, store):
        @pl.when(is_end)
        def _():
            got(j, m, 0)
            for k in range(nk[j]):
                store(k, rows_of(j, m, 0, k) + rx[j][m, 0, k * block:(k + 1) * block, :].astype(F32))

        @pl.when(is_mid)
        def _():
            got(j, m, 2)
            got(j, m, 4)
            for k in range(nk[j]):
                rows = slice(k * block, (k + 1) * block)
                store(k, rows_of(j, m, 1, k) + rx[j][m, 2, rows, :].astype(F32) + rx[j][m, 4, rows, :].astype(F32))

    def store_field0(k, value):
        fields[3 * c + mine, k * block:(k + 1) * block, :] = value.astype(BF16)

        @pl.when(x == k)
        def _():
            strips_ref[mine] = value

    def store_field1(k, value):
        fields[3 * c + 1, pl.ds(pl.multiple_of(x * block, 16), block), :] = value.astype(BF16)
        strips_ref[1] = value

    def store_g0(k, value):
        gfin0[k * block:(k + 1) * block, :] = value

    def store_g1(k, value):
        gfin1[...] = value

    swaps[0].wait_recv()
    set_trig(1, phx[...])
    for j in range(2):
        swaps[1 + 2 * j].wait_recv()
        swaps[2 + 2 * j].wait_recv()
        build(1, wx.at[j], vx.at[j])
        part[j, 0] += transposed_dot(left[...], right[0]) * scale_sites
        reduce_end(j, 0)
        reduce_mid(j, 0)
        part[j, 1] += transposed_dot(left[...], right[1]) * scale_sites
    for j in range(2):
        reduce_end(j, 1)

    half = pl.ds(pl.multiple_of(x * block, 16), block)
    half_peer = pl.ds(pl.multiple_of((1 - x) * block, 16), block)
    give0 = to(fields.at[3 * c + mine], fields.at[3 * c + mine], ms_sem.at[0], mr_sem.at[0], space=peer)
    give1 = to(fields.at[3 * c + 1, half], fields.at[3 * c + 1, half], ms_sem.at[1], mr_sem.at[1], space=peer)
    finish(0, 0, store_field0)
    give0.start()
    finish(1, 0, store_field1)
    give1.start()
    reduce_mid(0, 1)
    give0.wait_recv()
    give1.wait_recv()
    sibling = to(
        fields.at[pl.ds(3 * c, 3)], fields.at[pl.ds(3 * c, 3)], ts_sem.at[0], tr_sem.at[0], tm=1 - c
    )
    sibling.start()
    strips_ref[other] = fields[3 * c + other, half, :].astype(F32)
    reduce_mid(1, 1)
    sibling.wait_recv()

    def weight(t, k):
        at = 3 * c + t
        there = at + seq_ref[at]
        return jnp.where(jnp.logical_or(there == k, there == k + nslices), 1.0, 0.0)

    chosen0[...] = sum(weight(mine, k) * fields[k].astype(F32) for k in range(nslices))
    chosen1[...] = sum(weight(1, k) * fields[k, half, :].astype(F32) for k in range(nslices))
    finish(0, 1, store_g0)
    finish(1, 1, store_g1)

    def margins(g, field):
        gr, gi = g[:, :n], g[:, n:]
        mr, mi = field[:, :n], field[:, n:]
        re = jnp.sum(mr * gr - mi * gi, axis=1, keepdims=True) * scale_modes
        im = jnp.sum(mr * gi + mi * gr, axis=1, keepdims=True) * scale_modes
        return re, im

    cols[...] = jnp.zeros_like(cols)
    at = lax.broadcasted_iota(jnp.int32, (2 * block, 128), 1)
    re, im = margins(gfin0[...], chosen0[...])
    cols[:2 * block] = jnp.where(at == 0, re, 0.0) + jnp.where(at == 1, im, 0.0)
    re, im = margins(gfin1[...], chosen1[...])
    at = lax.broadcasted_iota(jnp.int32, (block, 128), 1)
    cols[half] += jnp.where(at == 2, re, 0.0) + jnp.where(at == 3, im, 0.0)
    tile[...] = jnp.transpose(cols[...])[:8]

    shares = []
    for k in range(1, nspace):
        share = to(tile, gathered.at[s], as_sem.at[k], ar_sem.at[s], space=(s + k) % nspace)
        share.start()
        shares.append(share)
    gathered[s] = tile[...]
    for k in range(1, nspace):
        origin = (s + k) % nspace
        to(tile, gathered.at[origin], as_sem.at[k], ar_sem.at[origin], space=origin).wait_recv()
    total = jnp.zeros((16, n), F32)
    for zz in range(nspace // 2):
        both = jnp.concatenate([gathered[2 * zz], gathered[2 * zz + 1]], axis=0)
        total += jnp.dot(both, place[zz], precision=lax.Precision.HIGHEST, preferred_element_type=F32)
    margin_ref[0:1, :n] = total[0:1]
    margin_ref[0:1, n:] = total[1:2]
    margin_ref[1:2, :n] = total[2:3] + total[10:11]
    margin_ref[1:2, n:] = total[3:4] + total[11:12]
    margin_ref[2:3, :n] = total[8:9]
    margin_ref[2:3, n:] = total[9:10]

    for swap in swaps:
        swap.wait_send()
    for j in range(2):
        for m in range(2):
            for slot in range(3):
                hop(j, m, slot, 0, z).wait_send()
    give0.wait_send()
    give1.wait_send()
    sibling.wait_send()
    for share in shares:
        share.wait_send()


def fused(w_modes, v_modes, phase_index, seq_offset, owner_block):
    tdev, sdev, width = w_modes.shape
    n = width // 2
    nspace = lax.axis_size("space")
    ntm = lax.axis_size("tm")
    block = n // nspace
    vmem = pl.BlockSpec(memory_space=pltpu.VMEM)
    hbm = pl.BlockSpec(memory_space=pltpu.HBM)
    smem = pl.BlockSpec(memory_space=pltpu.SMEM)
    dma = pltpu.SemaphoreType.DMA
    strips, margin = pl.pallas_call(
        functools.partial(kernel, tdev * ntm),
        out_shape=(
            jax.ShapeDtypeStruct((tdev, block, width), F32),
            jax.ShapeDtypeStruct((tdev, width), F32),
        ),
        in_specs=[hbm, hbm, vmem, smem, smem],
        out_specs=(vmem, vmem),
        scratch_shapes=[
            pltpu.VMEM((2, sdev, width), BF16),
            pltpu.VMEM((2, sdev, width), BF16),
            pltpu.VMEM((8, sdev), F32),
            pltpu.VMEM((8, sdev), F32),
            pltpu.VMEM((2, 2, sdev, sdev), F32),
            pltpu.VMEM((2 * sdev, n), BF16),
            pltpu.VMEM((2, 2 * sdev, width), BF16),
            pltpu.VMEM((2, 2, n, width), F32),
            pltpu.VMEM((2, 3, 2 * block, width), BF16),
            pltpu.VMEM((2, 3, block, width), BF16),
            pltpu.VMEM((2, 5, 2 * block, width), BF16),
            pltpu.VMEM((2, 5, block, width), BF16),
            pltpu.VMEM((tdev * ntm, 2 * block, width), BF16),
            pltpu.VMEM((2 * block, width), F32),
            pltpu.VMEM((block, width), F32),
            pltpu.VMEM((128, 128), F32),
            pltpu.VMEM((8, 128), F32),
            pltpu.VMEM((nspace, 8, 128), F32),
            pltpu.VMEM((nspace // 2, 128, n), F32),
            pltpu.VMEM((n, n), BF16),
            pltpu.VMEM((2 * block, width), F32),
            pltpu.VMEM((block, width), F32),
            pltpu.VMEM((2, sdev, width), BF16),
            pltpu.VMEM((2, sdev, width), BF16),
            dma((4,)),
            dma((5,)),
            dma((5,)),
            dma((2, 2, 3)),
            dma((2, 2, 5)),
            dma((2,)),
            dma((2,)),
            dma((1,)),
            dma((1,)),
            dma((nspace,)),
            dma((nspace,)),
        ],
        compiler_params=pltpu.CompilerParams(
            collective_id=0, has_side_effects=True, vmem_limit_bytes=60 * 1024 * 1024
        ),
        cost_estimate=pl.CostEstimate(
            flops=16 * tdev * sdev * n * n, bytes_accessed=4 * tdev * sdev * width, transcendentals=0
        ),
    )(w_modes, v_modes, phase_index.reshape(1, sdev), seq_offset, owner_block)
    return jnp.transpose(strips, (1, 0, 2)), margin


def plain(w_modes, v_modes, phase_index, seq_offset, owner_block):
    tdev, sdev, width = w_modes.shape
    nmode = width // 2
    nspace = lax.axis_size("space")
    ntm = lax.axis_size("tm")
    block = nmode // nspace
    total_slices = tdev * ntm
    scale_sites = 1.0 / math.sqrt(sdev * nspace)
    scale_modes = 1.0 / math.sqrt(2 * nmode)
    order = (owner_block[:, None] * block + jnp.arange(block, dtype=jnp.int32)[None, :]).reshape(-1)
    spots = order[:, None] == jnp.arange(nmode, dtype=jnp.int32)[None, :]
    hot = spots.astype(BF16)
    exact = spots.astype(F32)
    w_real = jnp.einsum("tsm,km->tsk", w_modes[:, :, :nmode], hot)
    w_imag = jnp.einsum("tsm,km->tsk", w_modes[:, :, nmode:], hot)
    v_real, v_imag = v_modes[:, :, :nmode], v_modes[:, :, nmode:]
    left = jnp.concatenate([w_real, w_imag], axis=1)
    angle = phase_index.astype(F32) * (2.0 * math.pi / PHASES)
    cosv = jnp.cos(angle)[None, :, None]
    sinv = jnp.sin(angle)[None, :, None]
    fr, fi = v_real.astype(F32), v_imag.astype(F32)
    ph_real = (cosv * fr + sinv * fi).astype(BF16)
    ph_imag = (cosv * fi - sinv * fr).astype(BF16)

    def field(real, imag):
        right = jnp.concatenate(
            [jnp.concatenate([real, imag], axis=2), jnp.concatenate([imag, -real], axis=2)], axis=1
        )
        sums = jnp.einsum("tsi,tsj->itj", left, right, preferred_element_type=F32) * scale_sites
        return lax.psum_scatter(sums, "space", scatter_dimension=0, tiled=True)

    strips = field(ph_real, ph_imag)
    g = field(v_real, v_imag)
    rounded = strips.astype(BF16)
    both = lax.all_gather(rounded, "tm", axis=1, tiled=True)
    mine = lax.axis_index("tm") * tdev + jnp.arange(tdev, dtype=jnp.int32)
    every = jnp.arange(total_slices, dtype=jnp.int32)
    offset = jnp.sum(jnp.where(mine[:, None] == every[None, :], seq_offset[None, :], 0), axis=1)
    target = (mine + offset) % total_slices
    pick = (target[:, None] == every[None, :]).astype(BF16)
    chosen = jnp.einsum("iaj,ta->itj", both, pick, preferred_element_type=F32)
    cr, ci = chosen[:, :, :nmode], chosen[:, :, nmode:]
    gr, gi = g[:, :, :nmode], g[:, :, nmode:]
    over = jnp.concatenate(
        [jnp.sum(cr * gr - ci * gi, axis=2), jnp.sum(cr * gi + ci * gr, axis=2)], axis=1
    ) * scale_modes
    rows = lax.all_gather(over, "space", axis=0, tiled=True)
    margin = jnp.einsum("kt,km->tm", rows, exact, precision=lax.Precision.HIGHEST)
    return strips, jnp.concatenate([margin[:tdev], margin[tdev:]], axis=1)


def shards(w_modes, v_modes, phase_index, seq_offset, owner_block):
    tdev, sdev, width = w_modes.shape
    nmode = width // 2
    nspace = lax.axis_size("space")
    fits = (
        tdev == 3 and lax.axis_size("tm") == 2 and nspace == 8 and sdev == 128
        and nmode % 128 == 0 and (nmode // nspace) % 16 == 0 and 2 * (nmode // nspace) <= 128
    )
    return (fused if fits else plain)(w_modes, v_modes, phase_index, seq_offset, owner_block)


def solution(mesh):
    in_specs = (
        P(("group", "tm"), "space", None),
        P(("group", "tm"), "space", None),
        P("space"),
        P(),
        P(),
    )
    out_specs = (P("space", ("group", "tm"), None), P(("group", "tm"), None))
    return jax.shard_map(shards, mesh=mesh, in_specs=in_specs, out_specs=out_specs, check_vma=False)
```
